32 devices in a mesh: row: 4 (over y, core), col: 8 (over z, x).
Axes of the slice: x: 2, y: 2, z: 4, core: 2. Of those that a mesh axis runs over, the one named last changes fastest.
Arguments:
- features: bfloat16 [8, 1024, 128], P('col', 'row'), may hold values from -6 to 6
- block_values: bfloat16 [4, 8, 64, 128, 128], P('row', 'col'), may hold values from -0.15625 to 0.15625
- block_row: int32 [4, 8, 64], P('row', 'col'), may hold values from 0 to 15
- block_col: int32 [4, 8, 64], P('row', 'col'), may hold values from 0 to 7
- block_occupancy: int32 [4, 8], P('row', 'col'), may hold values from 8 to 64, as said below
- weight: bfloat16 [128, 128], replicated, may hold values from -0.5 to 0.5
- cotangent: bfloat16 [4, 2048, 128], P('row', 'col'), may hold values from -6 to 6
Outputs:
- out_features: bfloat16 [4, 2048, 128], P('row', 'col')
- weight_grad: float32 [128, 128], replicated
- feature_grad: bfloat16 [8, 1024, 128], P('col', 'row')
The draws below stay inside these ranges and needn't reach their ends.
Inputs may be any that keep to these rules, and one draw needn't show every extreme that they name: `block_occupancy`: live slots of one tile name distinct blocks; some tile has all 64 slots live in every draw.
All inputs are finite; a program needn't handle non-finite values.
Results may differ from the reference program's by a relative error of at most 0.005.
Values may be sent and summed in bfloat16 or wider, within the bound.
No kernel may reach another device: no remote copies, remote signals or barrier semaphores. Data moves between devices by JAX's collectives and lax.ppermute only.
A program may use at most 192 MiB of HBM per device.

```python
import math
import jax
import jax.numpy as jnp
from jax import lax

F = 128
BLK = 128
NODES = 8192
ROWBLK = 2048
COLBLK = 1024
BROWS = 16
BCOLS = 8
NB = 64
N_ROW = 4
N_COL = 8


def tile_pattern(key):
    tile_count = N_ROW * N_COL
    slot_total = BROWS * BCOLS
    lowest = max(1, NB // 8)
    middle = max(lowest, NB // 2)
    base_key, heavy_key, pick_key, perm_key, top_key = jax.random.split(jax.random.fold_in(key, 7), 5)
    base_counts = jax.random.randint(base_key, (tile_count,), lowest, middle + 1)
    heavy_counts = jax.random.randint(heavy_key, (tile_count,), middle, NB + 1)
    heavy_pick = jax.random.randint(pick_key, (tile_count,), 0, 16) == 0
    counts = jnp.where(heavy_pick, heavy_counts, base_counts)
    top_tile = jax.random.randint(top_key, (), 0, tile_count)
    counts = jnp.where(jnp.arange(tile_count) == top_tile, NB, counts)
    tile_keys = jax.random.split(perm_key, tile_count)
    chosen = jax.vmap(lambda one_key: jax.random.permutation(one_key, slot_total)[:NB])(tile_keys)
    owned_rows_lookup = (chosen // BCOLS).astype(jnp.int32).reshape(N_ROW, N_COL, NB)
    cols_of = (chosen % BCOLS).astype(jnp.int32).reshape(N_ROW, N_COL, NB)
    return (counts.astype(jnp.int32).reshape(N_ROW, N_COL), owned_rows_lookup, cols_of)


def draw_block_occupancy(key, part):
    return tile_pattern(key)[0]


def draw_block_row(key, part):
    return tile_pattern(key)[1]


def draw_block_col(key, part):
    return tile_pattern(key)[2]


def shard_levels(rng, dims, pieces, low, high):
    factor_of = 1.0
    for dim, shards_of in pieces:
        draws = jax.random.uniform(jax.random.fold_in(jax.random.fold_in(rng, 6), dim), (shards_of,), jnp.float32, low / len(pieces), high / len(pieces))
        factor_of = factor_of * jnp.repeat(jnp.exp(draws), dims[dim] // shards_of).reshape((-1,) + (1,) * (len(dims) - 1 - dim))
    return factor_of


def normal_values(key, dims, deviation, limit, cuts=(), kind=jnp.bfloat16):
    drawn = jax.random.normal(key, dims, jnp.float32) * deviation
    if len(cuts) > 0:
        drawn = shard_levels(key, dims, cuts, -0.22, 0.18) * drawn
    return jnp.clip(drawn, min=-limit, max=limit).astype(kind)


def setup_inputs(seed: int = 0) -> dict:
    key_list = jax.random.split(jax.random.key(seed), 8)
    return {
        "features": normal_values(key_list[0], (N_COL, COLBLK, F), 1.0, 6.0, ((0, 8), (1, 4))),
        "block_values": normal_values(key_list[1], (N_ROW, N_COL, NB, BLK, BLK), (max(BLK, BLK * NB * N_COL // (3 * BROWS))) ** -0.5, 0.15625, ((0, 4), (1, 8))),
        "block_row": draw_block_row(jax.random.fold_in(key_list[7], 71), 0),
        "block_col": draw_block_col(jax.random.fold_in(key_list[7], 71), 0),
        "block_occupancy": draw_block_occupancy(jax.random.fold_in(key_list[7], 71), 0),
        "weight": normal_values(key_list[5], (F, F), F ** -0.5, 0.5),
        "cotangent": normal_values(key_list[6], (N_ROW, ROWBLK, F), 1.0, 6.0, ((0, 4), (1, 8))),
    }


def reference(features, block_values, block_row, block_col, block_occupancy, weight, cotangent):
    tile_count = N_ROW * N_COL
    tile_entries = block_values.reshape(tile_count, NB, BLK, BLK)
    tile_rows = block_row.reshape(tile_count, NB)
    tile_cols = block_col.reshape(tile_count, NB)
    tile_live = block_occupancy.reshape(tile_count)
    slot_index = jnp.arange(NB, dtype=jnp.int32)
    row_range = jnp.arange(BROWS, dtype=jnp.int32)
    col_range = jnp.arange(BCOLS, dtype=jnp.int32)
    tile_ids = jnp.arange(tile_count, dtype=jnp.int32)

    def forward(totals, tile_item):
        tile_id, values, owned_rows_lookup, cols_of, live_count = tile_item
        row_tile = tile_id // N_COL
        col_tile = tile_id % N_COL
        column_rows = lax.dynamic_index_in_dim(features, col_tile, 0, keepdims=False)
        picked = column_rows.reshape(BCOLS, BLK, F)[cols_of].astype(jnp.float32)
        tile_multiplied = jnp.einsum('sab,sbf->saf', values.astype(jnp.float32), picked, precision=lax.Precision.HIGHEST)
        live_mask = (slot_index < live_count).astype(jnp.float32)
        select_rows = (owned_rows_lookup[:, None] == row_range[None, :]).astype(jnp.float32) * live_mask[:, None]
        partial_output = jnp.einsum('sr,saf->raf', select_rows, tile_multiplied, precision=lax.Precision.HIGHEST)
        return (totals.at[row_tile].add(partial_output.reshape(ROWBLK, F)), None)
    agg_sum = lax.scan(forward, jnp.zeros((N_ROW, ROWBLK, F), jnp.float32), (tile_ids, tile_entries, tile_rows, tile_cols, tile_live))[0]
    neighbor_total = agg_sum.astype(jnp.bfloat16).reshape(NODES, F)
    out_features = jnp.dot(neighbor_total, weight, preferred_element_type=jnp.float32).astype(jnp.bfloat16)
    cot_flat = cotangent.reshape(NODES, F)
    weight_grad = jnp.dot(neighbor_total.T, cot_flat, preferred_element_type=jnp.float32) * (1.0 / math.sqrt(NODES))
    grad_agg = jnp.dot(cot_flat, weight.T, preferred_element_type=jnp.float32).astype(jnp.bfloat16)
    grad_tiles = grad_agg.reshape(N_ROW, BROWS, BLK, F)

    def backward(totals, tile_item):
        tile_id, values, owned_rows_lookup, cols_of, live_count = tile_item
        row_tile = tile_id // N_COL
        col_tile = tile_id % N_COL
        grad_rows = lax.dynamic_index_in_dim(grad_tiles, row_tile, 0, keepdims=False)
        picked = grad_rows[owned_rows_lookup].astype(jnp.float32)
        tile_multiplied = jnp.einsum('sab,saf->sbf', values.astype(jnp.float32), picked, precision=lax.Precision.HIGHEST)
        live_mask = (slot_index < live_count).astype(jnp.float32)
        gather_columns = (cols_of[:, None] == col_range[None, :]).astype(jnp.float32) * live_mask[:, None]
        partial_output = jnp.einsum('wx,wyn->xyn', gather_columns, tile_multiplied, precision=lax.Precision.HIGHEST)
        return (totals.at[col_tile].add(partial_output.reshape(COLBLK, F)), None)
    grad_sum = lax.scan(backward, jnp.zeros((N_COL, COLBLK, F), jnp.float32), (tile_ids, tile_entries, tile_rows, tile_cols, tile_live))[0]
    feature_grad = grad_sum.astype(jnp.bfloat16)
    return (out_features.reshape(N_ROW, ROWBLK, F), weight_grad, feature_grad)
```

```python
import functools
import math

import jax
import jax.numpy as jnp
from jax import lax
from jax.experimental import pallas as pl
from jax.experimental.pallas import tpu as pltpu
from jax.sharding import PartitionSpec as P

F32 = jnp.float32
BF16 = jnp.bfloat16
VMEM = pl.BlockSpec(memory_space=pltpu.VMEM)
SMEM = pl.BlockSpec(memory_space=pltpu.SMEM)
ANY = pl.BlockSpec(memory_space=pl.ANY)


def call(body, outs, ins, operands, scratch=(), flops=0, name=None):
    sizes = [math.prod(o.shape) * o.dtype.itemsize for o in outs]
    sizes += [math.prod(o.shape) * o.dtype.itemsize for o in operands]
    return pl.pallas_call(
        body,
        out_shape=outs,
        in_specs=ins,
        out_specs=[VMEM] * len(outs),
        scratch_shapes=scratch,
        compiler_params=pltpu.CompilerParams(vmem_limit_bytes=56 * 1024 * 1024),
        cost_estimate=pl.CostEstimate(flops=flops, bytes_accessed=sum(sizes), transcendentals=0),
        name=name,
    )(*operands)


def sds(shape, dtype):
    return jax.ShapeDtypeStruct(shape, dtype)


def densify(rows_ref, cols_ref, live_ref, values_ref, tile_ref, sems):
    block = values_ref.shape[1]
    live = live_ref[0, 0]

    def clear(i, carry):
        tile_ref[pl.ds(i * block, block), :] = jnp.zeros((block, tile_ref.shape[1]), tile_ref.dtype)
        return carry

    lax.fori_loop(0, tile_ref.shape[0] // block, clear, 0)

    def copy(s):
        r = pl.multiple_of(rows_ref[0, 0, s] * block, block)
        c = pl.multiple_of(cols_ref[0, 0, s] * block, block)
        return pltpu.make_async_copy(
            values_ref.at[s], tile_ref.at[pl.ds(r, block), pl.ds(c, block)], sems.at[s]
        )

    def start(s, carry):
        copy(s).start()
        return carry

    def wait(s, carry):
        copy(s).wait()
        return carry

    lax.fori_loop(0, live, start, 0)
    lax.fori_loop(0, live, wait, 0)


def aggregate(n_row, n_col, own, *refs):
    parts, tile_ref = refs[:n_row], refs[n_row]
    keep_ref, send_ref, whole = refs[n_row + 1 :]
    sub = own
    row, col = lax.axis_index("row"), lax.axis_index("col")
    for k in range(n_row):
        whole[pl.ds(pl.multiple_of((row ^ k) * sub, sub), sub), :] = parts[k][...]
    for k in range(n_col):
        start = pl.multiple_of((col ^ k) * sub, sub)
        part = jnp.dot(tile_ref[pl.ds(start, sub), :], whole[...], preferred_element_type=F32)
        if k % 2:
            send_ref[k // 2] = part.astype(BF16)
        else:
            keep_ref[k // 2] = part


def gradients(n_row, n_col, scale, *refs):
    cots = refs[:n_col]
    tile_ref, keep_ref, send_ref, weight_ref, q_keep, q_send, w_ref, total = refs[n_col:]
    sub = cots[0].shape[0]
    row, col = lax.axis_index("row"), lax.axis_index("col")
    weight = weight_ref[...]
    w_total = jnp.zeros(w_ref.shape, F32)
    for k in range(n_col):
        start = pl.multiple_of((col ^ k) * sub, sub)
        cot = cots[k][...].T
        grad = jnp.dot(weight, cot, preferred_element_type=F32).astype(BF16)
        part = send_ref[k // 2] if k % 2 else keep_ref[k // 2].astype(BF16)
        w_total += jnp.dot(cot, part, preferred_element_type=F32)
        term = jnp.dot(grad, tile_ref[pl.ds(start, sub), :], preferred_element_type=F32)
        if k:
            total[...] += term
        else:
            total[...] = term
    w_ref[...] = w_total.T * scale
    for k in range(n_row):
        start = pl.multiple_of((row ^ k) * sub, sub)
        piece = total[:, pl.ds(start, sub)]
        if k % 2:
            q_send[k // 2] = piece
        else:
            q_keep[k // 2] = piece


def add_pairs(keep_ref, got_ref, own_ref, *send_refs):
    own_ref[...] = keep_ref[0] + got_ref[0].astype(F32)
    for k, ref in enumerate(send_refs):
        ref[...] = (keep_ref[k + 1] + got_ref[k + 1].astype(F32)).astype(BF16)


def finish_out(own_ref, weight_ref, *refs):
    total = own_ref[...]
    for ref in refs[:-1]:
        total += ref[...].astype(F32)
    refs[-1][0] = jnp.dot(total.astype(BF16), weight_ref[...], preferred_element_type=F32).astype(BF16)


def finish_grad(own_ref, *refs):
    total = own_ref[...]
    for ref in refs[:-1]:
        total += ref[...].astype(F32)
    refs[-1][0] = total.T.astype(BF16)


def local(features, block_values, block_row, block_col, block_occupancy, weight, cotangent):
    n_row, n_col = lax.axis_size("row"), lax.axis_size("col")
    sub, width = features.shape[1:]
    slots, block = block_values.shape[2:4]
    rows, cols = n_col * sub, n_row * sub
    x_own, c_own = features[0], cotangent[0]

    def move(x, axis, k):
        n = lax.axis_size(axis)
        return lax.ppermute(x, axis, [(i, i ^ k) for i in range(n)])

    def device(row, col):
        return row * n_col + col

    def hub(x, row_k, col_k):
        pairs = [
            (device(r, c), device(r ^ row_k, c ^ col_k))
            for r in range(1, n_row, 2)
            for c in range(n_col)
        ]
        return lax.ppermute(x, ("row", "col"), pairs)

    x_parts = [None] * n_row
    x_parts[0] = x_own
    for k in range(2, n_row, 2):
        x_parts[k] = move(x_own, "row", k)
    for k in range(0, n_row, 2):
        x_parts[k + 1] = move(x_parts[k], "row", 1)
    c_parts = [c_own] + [None] * (n_col - 1)
    for k in list(range(n_col - 1, 0, -1)):
        c_parts[k] = move(c_own, "col", k)

    (tile,) = call(
        densify,
        [sds((rows, cols), BF16)],
        [SMEM, SMEM, SMEM, ANY],
        [block_row, block_col, block_occupancy, block_values[0, 0]],
        [pltpu.SemaphoreType.DMA((slots,))],
        name="densify",
    )
    keep, send = call(
        functools.partial(aggregate, n_row, n_col, sub),
        [sds((n_col // 2, sub, width), F32), sds((n_col // 2, sub, width), BF16)],
        [VMEM] * (n_row + 1),
        [*x_parts, tile],
        [pltpu.VMEM((cols, width), BF16)],
        flops=2 * rows * cols * width,
        name="aggregate",
    )
    got = move(send, "col", 1)
    q_keep, q_send, w_part = call(
        functools.partial(gradients, n_row, n_col, 1.0 / math.sqrt(n_row * rows)),
        [
            sds((n_row // 2, width, sub), F32),
            sds((n_row // 2, width, sub), F32),
            sds((width, width), F32),
        ],
        [VMEM] * (n_col + 4),
        [*c_parts, tile, keep, send, weight],
        [pltpu.VMEM((width, cols), F32)],
        flops=2 * rows * cols * width,
        name="gradients",
    )

    core_pairs = [(device(r, c), device(r + 1, c)) for r in range(0, n_row, 2) for c in range(n_col)]
    w_total = w_part + lax.ppermute(w_part, ("row", "col"), core_pairs)
    k = 2
    while k < n_row:
        w_total = w_total + hub(w_total, k, 0)
        k *= 2
    k = 1
    while k < n_col:
        w_total = w_total + hub(w_total, 0, k)
        k *= 2
    w_back = lax.ppermute(w_total, ("row", "col"), [(b, a) for a, b in core_pairs])
    weight_grad = jnp.where(lax.axis_index("row") % 2 == 1, w_total, w_back)

    p_own, *p_send = call(
        add_pairs,
        [sds((sub, width), F32)] + [sds((sub, width), BF16)] * (n_col // 2 - 1),
        [VMEM] * 2,
        [keep, got],
        name="add_x",
    )
    p_got = [move(x, "col", 2 * (k + 1)) for k, x in enumerate(p_send)]
    q_got = move(q_send, "row", 1)
    q_own, *q_out = call(
        add_pairs,
        [sds((width, sub), F32)] + [sds((width, sub), BF16)] * (n_row // 2 - 1),
        [VMEM] * 2,
        [q_keep, q_got],
        name="add_core",
    )
    q_in = [move(x, "row", 2 * (k + 1)) for k, x in enumerate(q_out)]
    (out_rows,) = call(
        finish_out,
        [sds((1, sub, width), BF16)],
        [VMEM] * (2 + len(p_got)),
        [p_own, weight, *p_got],
        name="finish_out",
    )
    (feature_grad,) = call(
        finish_grad,
        [sds((1, sub, width), BF16)],
        [VMEM] * (1 + len(q_in)),
        [q_own, *q_in],
        name="finish_grad",
    )
    return out_rows, weight_grad, feature_grad


def solution(mesh):
    in_specs = (
        P("col", "row", None),
        P("row", "col", None, None, None),
        P("row", "col", None),
        P("row", "col", None),
        P("row", "col"),
        P(),
        P("row", "col", None),
    )
    out_specs = (P("row", "col", None), P(), P("col", "row", None))
    return jax.shard_map(local, mesh=mesh, in_specs=in_specs, out_specs=out_specs, check_vma=False)
```

```python
import functools
import math

import jax
import jax.numpy as jnp
from jax import lax
from jax.experimental import pallas as pl
from jax.experimental.pallas import tpu as pltpu
from jax.sharding import PartitionSpec as P

F32 = jnp.float32
BF16 = jnp.bfloat16
VMEM = pl.BlockSpec(memory_space=pltpu.VMEM)
SMEM = pl.BlockSpec(memory_space=pltpu.SMEM)
HBM = pl.BlockSpec(memory_space=pltpu.HBM)


def call(body, outs, ins, operands, scratch=(), flops=0, name=None):
    sizes = [math.prod(o.shape) * o.dtype.itemsize for o in outs]
    sizes += [math.prod(o.shape) * o.dtype.itemsize for o in operands]
    limit = sum(sizes) + sum(math.prod(s.shape) * 4 for s in scratch) + 2 * 1024 * 1024
    return pl.pallas_call(
        body,
        out_shape=outs,
        in_specs=ins,
        out_specs=[VMEM] * len(outs),
        scratch_shapes=scratch,
        compiler_params=pltpu.CompilerParams(vmem_limit_bytes=limit),
        cost_estimate=pl.CostEstimate(flops=flops, bytes_accessed=sum(sizes), transcendentals=0),
        name=name,
    )(*operands)


def sds(shape, dtype):
    return jax.ShapeDtypeStruct(shape, dtype)


def densify(rows_hbm, cols_hbm, live_hbm, values_hbm, *refs):
    count = (len(refs) - 6) // 2
    tile_ref = refs[count]
    rows_ref, cols_ref, live_ref, sems, few = refs[2 * count + 1 :]
    block = values_hbm.shape[3]
    slots = zip((rows_hbm, cols_hbm, live_hbm), (rows_ref, cols_ref, live_ref))
    first = [pltpu.make_async_copy(a, b, few.at[i]) for i, (a, b) in enumerate(slots)]
    passed = zip(refs[:count], refs[count + 1 : 2 * count + 1])
    later = [pltpu.make_async_copy(a, b, few.at[i + 3]) for i, (a, b) in enumerate(passed)]
    for one in first + later:
        one.start()

    def clear(i, carry):
        tile_ref[pl.ds(i * block, block), :] = jnp.zeros((block, tile_ref.shape[1]), tile_ref.dtype)
        return carry

    lax.fori_loop(0, tile_ref.shape[0] // block, clear, 0)
    for one in first:
        one.wait()
    live = live_ref[0, 0]

    def copy(s):
        r = pl.multiple_of(rows_ref[0, 0, s] * block, block)
        c = pl.multiple_of(cols_ref[0, 0, s] * block, block)
        return pltpu.make_async_copy(
            values_hbm.at[0, 0, s], tile_ref.at[pl.ds(r, block), pl.ds(c, block)], sems.at[s]
        )

    def start(s, carry):
        copy(s).start()
        return carry

    def wait(s, carry):
        copy(s).wait()
        return carry

    lax.fori_loop(0, live, start, 0)
    lax.fori_loop(0, live, wait, 0)
    for one in later:
        one.wait()


def join(*refs):
    for k, ref in enumerate(refs[:-1]):
        refs[-1][k] = ref[...]


def aggregate(n_row, n_col, own, *refs):
    parts, tile_ref = refs[:n_row], refs[n_row]
    keep_ref, send_ref, whole = refs[n_row + 1 :]
    sub = own
    row, col = lax.axis_index("row"), lax.axis_index("col")
    for k in range(n_row):
        whole[pl.ds(pl.multiple_of((row ^ k) * sub, sub), sub), :] = parts[k][...]
    for k in range(n_col):
        start = pl.multiple_of((col ^ k) * sub, sub)
        part = jnp.dot(tile_ref[pl.ds(start, sub), :], whole[...], preferred_element_type=F32)
        if k % 2:
            send_ref[k // 2] = part.astype(BF16)
        else:
            keep_ref[k // 2] = part


def gradients(n_row, n_col, scale, *refs):
    deep = n_col // 2
    half = deep // 2
    cots, sides = refs[:deep], refs[deep : deep + 2]
    tile_ref, keep_ref, send_ref, weight_ref, q_keep, q_send, w_ref, total = refs[deep + 2 :]
    sub = cots[0].shape[0]
    row, col = lax.axis_index("row"), lax.axis_index("col")
    weight = weight_ref[...]
    w_total = jnp.zeros(w_ref.shape, F32)
    for k in range(n_col):
        start = pl.multiple_of((col ^ k) * sub, sub)
        near = k // 2
        cot = (sides[near // half][near % half] if k % 2 else cots[near][...]).T
        grad = jnp.dot(weight, cot, preferred_element_type=F32).astype(BF16)
        part = send_ref[k // 2] if k % 2 else keep_ref[k // 2].astype(BF16)
        w_total += jnp.dot(cot, part, preferred_element_type=F32)
        term = jnp.dot(grad, tile_ref[pl.ds(start, sub), :], preferred_element_type=F32)
        if k:
            total[...] += term
        else:
            total[...] = term
    w_ref[...] = w_total.T * scale
    for k in range(n_row):
        start = pl.multiple_of((row ^ k) * sub, sub)
        piece = total[:, pl.ds(start, sub)]
        if k % 2:
            q_send[k // 2] = piece
        else:
            q_keep[k // 2] = piece


def add_pairs(keep_ref, got_ref, own_ref, *send_refs):
    own_ref[...] = keep_ref[0] + got_ref[0].astype(F32)
    for k, ref in enumerate(send_refs):
        ref[...] = (keep_ref[k + 1] + got_ref[k + 1].astype(F32)).astype(BF16)


def add_pass(count, *refs):
    outs = refs[2 + count :]
    outs[0][...] = refs[0][...] + refs[1][...]
    for k in range(count):
        outs[1 + k][...] = refs[2 + k][...]


def finish_out(own_ref, weight_ref, *refs):
    total = own_ref[...]
    for ref in refs[:-1]:
        total += ref[...].astype(F32)
    refs[-1][0] = jnp.dot(total.astype(BF16), weight_ref[...], preferred_element_type=F32).astype(BF16)


def finish_grad(own_ref, *refs):
    total = own_ref[...]
    for ref in refs[:-1]:
        total += ref[...].astype(F32)
    refs[-1][0] = total.T.astype(BF16)


def local(features, block_values, block_row, block_col, block_occupancy, weight, cotangent):
    n_row, n_col = lax.axis_size("row"), lax.axis_size("col")
    sub, width = features.shape[1:]
    slots, block = block_values.shape[2:4]
    rows, cols = n_col * sub, n_row * sub
    x_own, c_own = features[0], cotangent[0]

    def move(x, axis, k):
        n = lax.axis_size(axis)
        return lax.ppermute(x, axis, [(i, i ^ k) for i in range(n)])

    def device(row, col):
        return row * n_col + col

    def hub(x, row_k, col_k):
        pairs = [
            (device(r, c), device(r ^ row_k, c ^ col_k))
            for r in range(1, n_row, 2)
            for c in range(n_col)
        ]
        return lax.ppermute(x, ("row", "col"), pairs)

    deep = n_col // 2
    half = deep // 2
    c_deep = [None] * deep
    for k in [*range(1, half), *range(deep - 1, half - 1, -1)]:
        c_deep[k] = move(c_own, "col", 2 * k)
    x_parts = [None] * n_row
    for k in range(2, n_row, 2):
        x_parts[k] = move(x_own, "row", k)
    def far(x):
        return pltpu.with_memory_space_constraint(x, pltpu.HBM)

    tile, c_deep[0], x_parts[0], w_near = call(
        densify,
        [sds((rows, cols), BF16), sds((sub, width), BF16), sds((sub, width), BF16), sds((width, width), BF16)],
        [HBM] * 7,
        [block_row, block_col, block_occupancy, *map(far, (block_values, c_own, x_own, weight))],
        [
            pltpu.SMEM(block_row.shape, jnp.int32),
            pltpu.SMEM(block_row.shape, jnp.int32),
            pltpu.SMEM(block_occupancy.shape, jnp.int32),
            pltpu.SemaphoreType.DMA((slots,)),
            pltpu.SemaphoreType.DMA((6,)),
        ],
        name="densify",
    )
    for k in range(0, n_row, 2):
        x_parts[k + 1] = move(x_parts[k], "row", 1)
    c_side = []
    for parts in (c_deep[:half], c_deep[half:]):
        (joined,) = call(
            join,
            [sds((half, sub, width), BF16)],
            [VMEM] * half,
            parts,
            name="join",
        )
        c_side.append(move(joined, "col", 1))
    keep, send = call(
        functools.partial(aggregate, n_row, n_col, sub),
        [sds((n_col // 2, sub, width), F32), sds((n_col // 2, sub, width), BF16)],
        [VMEM] * (n_row + 1),
        [*x_parts, tile],
        [pltpu.VMEM((cols, width), BF16)],
        flops=2 * rows * cols * width,
        name="aggregate",
    )
    got = move(send, "col", 1)
    q_keep, q_send, w_part = call(
        functools.partial(gradients, n_row, n_col, 1.0 / math.sqrt(n_row * rows)),
        [
            sds((n_row // 2, width, sub), F32),
            sds((n_row // 2, width, sub), F32),
            sds((width, width), F32),
        ],
        [VMEM] * (deep + 6),
        [*c_deep, *c_side, tile, keep, send, w_near],
        [pltpu.VMEM((width, cols), F32)],
        flops=2 * rows * cols * width,
        name="gradients",
    )

    w_got = move(w_part, "row", 1)
    q_got = move(q_send, "row", 1)
    p_own, *p_send = call(
        add_pairs,
        [sds((sub, width), F32)] + [sds((sub, width), BF16)] * (deep - 1),
        [VMEM] * 2,
        [keep, got],
        name="add_x",
    )
    q_own, *q_out = call(
        add_pairs,
        [sds((width, sub), F32)] + [sds((width, sub), BF16)] * (n_row // 2 - 1),
        [VMEM] * 2,
        [q_keep, q_got],
        name="add_core",
    )
    q_in = [move(x, "row", 2 * (k + 1)) for k, x in enumerate(q_out)]

    def add_w(mine, got, passed):
        operands = [mine, got, *passed]
        return call(
            functools.partial(add_pass, len(passed)),
            [sds(x.shape, x.dtype) for x in operands[1:]],
            [VMEM] * len(operands),
            operands,
            name="add_w",
        )

    (w_total,) = add_w(w_part, w_got, [])
    steps = [("row", 2**i) for i in range(1, n_row.bit_length() - 1)]
    steps += [("col", 2**i) for i in range(n_col.bit_length() - 1)]
    waiting = list(enumerate(p_send))
    p_got = [None] * len(waiting)
    for i, (axis, k) in enumerate(steps):
        w_got = move(w_total, axis, k)
        left = len(steps) - 1 - i
        count = -(-len(waiting) // left) if left else 0
        now, waiting = waiting[len(waiting) - count :], waiting[: len(waiting) - count]
        w_total, *passed = add_w(w_total, w_got, [x for _, x in now])
        for (j, _), x in zip(now, passed):
            p_got[j] = move(x, "col", 2 * (j + 1))
    weight_grad = w_total

    (out_rows,) = call(
        finish_out,
        [sds((1, sub, width), BF16)],
        [VMEM] * (2 + len(p_got)),
        [p_own, w_near, *p_got],
        name="finish_out",
    )
    (feature_grad,) = call(
        finish_grad,
        [sds((1, sub, width), BF16)],
        [VMEM] * (1 + len(q_in)),
        [q_own, *q_in],
        name="finish_grad",
    )
    return out_rows, weight_grad, feature_grad


def solution(mesh):
    in_specs = (
        P("col", "row", None),
        P("row", "col", None, None, None),
        P("row", "col", None),
        P("row", "col", None),
        P("row", "col"),
        P(),
        P("row", "col", None),
    )
    out_specs = (P("row", "col", None), P(), P("col", "row", None))
    return jax.shard_map(local, mesh=mesh, in_specs=in_specs, out_specs=out_specs, check_vma=False)
```

```python
import functools
import math

import jax
import jax.numpy as jnp
from jax import lax
from jax.experimental import pallas as pl
from jax.experimental.pallas import tpu as pltpu
from jax.sharding import PartitionSpec as P

F32 = jnp.float32
BF16 = jnp.bfloat16
VMEM = pl.BlockSpec(memory_space=pltpu.VMEM)
SMEM = pl.BlockSpec(memory_space=pltpu.SMEM)
HBM = pl.BlockSpec(memory_space=pltpu.HBM)


def call(body, outs, ins, operands, scratch=(), flops=0, name=None):
    sizes = [math.prod(o.shape) * o.dtype.itemsize for o in outs]
    sizes += [math.prod(o.shape) * o.dtype.itemsize for o in operands]
    limit = sum(sizes) + sum(math.prod(s.shape) * 4 for s in scratch) + 2 * 1024 * 1024
    return pl.pallas_call(
        body,
        out_shape=outs,
        in_specs=ins,
        out_specs=[VMEM] * len(outs),
        scratch_shapes=scratch,
        compiler_params=pltpu.CompilerParams(vmem_limit_bytes=limit),
        cost_estimate=pl.CostEstimate(flops=flops, bytes_accessed=sum(sizes), transcendentals=0),
        name=name,
    )(*operands)


def sds(shape, dtype):
    return jax.ShapeDtypeStruct(shape, dtype)


def join(token_ref, side_ref, *refs):
    for k, ref in enumerate(refs[:-1]):
        refs[-1][k] = ref[...]


def densify(live_ref, rows_hbm, cols_hbm, values_hbm, *refs):
    count = (len(refs) - 5) // 2
    tile_ref = refs[count]
    rows_ref, cols_ref, sems, few = refs[2 * count + 1 :]
    block = values_hbm.shape[3]
    pairs = ((rows_hbm, rows_ref), (cols_hbm, cols_ref))
    pairs += tuple(zip(refs[:count], refs[count + 1 : 2 * count + 1]))
    copies = [pltpu.make_async_copy(a, b, few.at[i]) for i, (a, b) in enumerate(pairs)]
    for one in copies:
        one.start()

    def clear(i, carry):
        tile_ref[pl.ds(i * block, block), :] = jnp.zeros((block, tile_ref.shape[1]), tile_ref.dtype)
        return carry

    lax.fori_loop(0, tile_ref.shape[0] // block, clear, 0)
    for one in copies[:2]:
        one.wait()
    live = live_ref[0, 0]

    def copy(s):
        r = pl.multiple_of(rows_ref[0, 0, s] * block, block)
        c = pl.multiple_of(cols_ref[0, 0, s] * block, block)
        return pltpu.make_async_copy(
            values_hbm.at[0, 0, s], tile_ref.at[pl.ds(r, block), pl.ds(c, block)], sems.at[s]
        )

    def start(s, carry):
        copy(s).start()
        return carry

    def wait(s, carry):
        copy(s).wait()
        return carry

    lax.fori_loop(0, live, start, 0)
    for one in copies[2:]:
        one.wait()
    lax.fori_loop(0, live, wait, 0)


def aggregate(n_row, n_col, tile_ref, *refs):
    parts = refs[:n_row]
    keep_ref, send_ref, whole = refs[n_row:]
    sub = parts[0].shape[0]
    row, col = lax.axis_index("row"), lax.axis_index("col")
    for k in range(n_row):
        whole[pl.ds(pl.multiple_of((row ^ k) * sub, sub), sub), :] = parts[k][...]
    for k in range(n_col):
        begin = pl.multiple_of((col ^ k) * sub, sub)
        part = jnp.dot(tile_ref[pl.ds(begin, sub), :], whole[...], preferred_element_type=F32)
        if k % 2:
            send_ref[k // 2] = part.astype(BF16)
        else:
            keep_ref[k // 2] = part


def own_half(rows):
    bits = (lax.axis_index("row"), lax.axis_index("col"))
    parity = 0
    for index, axis in zip(bits, ("row", "col")):
        for b in range(lax.axis_size(axis).bit_length() - 1):
            parity = parity ^ ((index >> b) & 1)
    mine = pl.multiple_of(parity * rows, rows)
    return pl.ds(mine, rows), pl.ds(pl.multiple_of(rows - mine, rows), rows)


def cotangent_of(refs, z):
    return (refs[1][z - 1] if z else refs[0][...]).T


def weight_term(n_col, scale, *refs):
    keep_ref, send_ref, token_ref, mine_ref, other_ref, whole = refs[4:]
    total = jnp.zeros(whole.shape, F32)
    for z in range(n_col // 2):
        for side in range(2):
            part = send_ref[z] if side else keep_ref[z].astype(BF16)
            cot = cotangent_of(refs[2 * side : 2 * side + 2], z)
            total += jnp.dot(cot, part, preferred_element_type=F32)
    whole[...] = total.T * scale
    mine, other = own_half(mine_ref.shape[0])
    mine_ref[...] = whole[mine, :]
    other_ref[...] = whole[other, :]


def finish_weight(mine_ref, other_ref, out_ref):
    mine, other = own_half(mine_ref.shape[0])
    out_ref[mine, :] = mine_ref[...]
    out_ref[other, :] = other_ref[...]


def feature_terms(n_col, side, own_ref, far_ref, tile_ref, weight_ref, *refs):
    total_ref, before_ref = refs[-1], refs[0] if side else None
    sub = own_ref.shape[0]
    col = lax.axis_index("col")
    weight = weight_ref[...]
    for z in range(n_col // 2):
        begin = pl.multiple_of((col ^ (2 * z + side)) * sub, sub)
        cot = cotangent_of((own_ref, far_ref), z)
        grad = jnp.dot(weight, cot, preferred_element_type=F32).astype(BF16)
        term = jnp.dot(grad, tile_ref[pl.ds(begin, sub), :], preferred_element_type=F32)
        if z > 0:
            total_ref[...] += term
        elif before_ref is not None:
            total_ref[...] = before_ref[...] + term
        else:
            total_ref[...] = term


def cut(n_row, total_ref, token_ref, q_keep, q_send):
    sub = q_keep.shape[2]
    row = lax.axis_index("row")
    for k in range(n_row):
        begin = pl.multiple_of((row ^ k) * sub, sub)
        piece = total_ref[:, pl.ds(begin, sub)]
        if (k + (k > 1)) % 2:
            q_send[k // 2] = piece
        else:
            q_keep[k // 2] = piece


def add_pairs(keep_ref, got_ref, own_ref, *send_refs):
    own_ref[...] = keep_ref[0] + got_ref[0].astype(F32)
    for k, ref in enumerate(send_refs):
        ref[...] = (keep_ref[k + 1] + got_ref[k + 1].astype(F32)).astype(BF16)


def add_two(a_ref, b_ref, *refs):
    refs[-1][...] = a_ref[...] + b_ref[...]


def add_last(after_ref, a_ref, b_ref, *refs):
    refs[-2][...] = a_ref[...] + b_ref[...]
    total = refs[0][...]
    for ref in refs[-3:0:-1]:
        total += ref[...].astype(F32)
    refs[-1][...] = total.astype(BF16)


def finish_out(total_ref, weight_ref, out_ref):
    out_ref[0] = jnp.dot(total_ref[...], weight_ref[...], preferred_element_type=F32).astype(BF16)


def finish_grad(own_ref, *refs):
    total = own_ref[...]
    for ref in refs[:-1]:
        total += ref[...].astype(F32)
    refs[-1][0] = total.T.astype(BF16)


def local(features, block_values, block_row, block_col, block_occupancy, weight, cotangent):
    n_row, n_col = lax.axis_size("row"), lax.axis_size("col")
    sub, width = features.shape[1:]
    slots, block = block_values.shape[2:4]
    rows, cols = n_col * sub, n_row * sub
    x_own, c_own = features[0], cotangent[0]

    def move(x, axis, k):
        n = lax.axis_size(axis)
        return lax.ppermute(x, axis, [(i, i ^ k) for i in range(n)])

    def far(x):
        return pltpu.with_memory_space_constraint(x, pltpu.HBM)

    deep = n_col // 2
    c_side = move(c_own, "col", 1)
    c_deep = [move(c_own, "col", 2 * k) for k in range(1, deep)]
    tile, c_near, w_near, x_near = call(
        densify,
        [
            sds((rows, cols), BF16),
            sds((sub, width), BF16),
            sds((width, width), BF16),
            sds((sub, width), BF16),
        ],
        [SMEM] + [HBM] * 6,
        [block_occupancy, *map(far, (block_row, block_col, block_values, c_own, weight, x_own))],
        [
            pltpu.SMEM(block_row.shape, jnp.int32),
            pltpu.SMEM(block_row.shape, jnp.int32),
            pltpu.SemaphoreType.DMA((slots,)),
            pltpu.SemaphoreType.DMA((5,)),
        ],
        name="densify",
    )
    (c_far,) = call(
        join,
        [sds((deep - 1, sub, width), BF16)],
        [VMEM] * (deep + 1),
        [w_near, c_side, *c_deep],
        name="join",
    )
    c_side = [c_side, move(c_far, "col", 1)]
    x_far = [move(x_near, "row", k) for k in range(3, n_row, 2)]
    x_parts = [x_near, move(x_near, "row", 1)]
    for x in x_far:
        x_parts += [move(x, "row", 1), x]
    keep, send = call(
        functools.partial(aggregate, n_row, n_col),
        [sds((deep, sub, width), F32), sds((deep, sub, width), BF16)],
        [VMEM] * (n_row + 1),
        [tile, *x_parts],
        [pltpu.VMEM((cols, width), BF16)],
        flops=2 * rows * cols * width,
        name="aggregate",
    )
    c_own_side = [c_near, c_far]
    (q_near,) = call(
        functools.partial(feature_terms, n_col, 0),
        [sds((width, cols), F32)],
        [VMEM] * 4,
        [*c_own_side, tile, w_near],
        flops=rows * cols * width,
        name="feature_near",
    )
    got = move(send, "col", 1)
    w_part, w_other = call(
        functools.partial(weight_term, n_col, 1.0 / math.sqrt(n_row * rows)),
        [sds((width // 2, width), F32)] * 2,
        [VMEM] * 7,
        [*c_own_side, *c_side, keep, send, q_near],
        [pltpu.VMEM((width, width), F32)],
        flops=2 * rows * width * width,
        name="weight_term",
    )
    def add_w(mine, got):
        (total,) = call(add_two, [sds(mine.shape, F32)], [VMEM] * 2, [mine, got], name="add_w")
        return total

    w_total = add_w(w_part, move(w_other, "row", 1))
    (q_total,) = call(
        functools.partial(feature_terms, n_col, 1),
        [sds((width, cols), F32)],
        [VMEM] * 6,
        [*c_side, tile, w_near, q_near, w_total],
        flops=rows * cols * width,
        name="feature_side",
    )
    p_own, *p_send = call(
        add_pairs,
        [sds((sub, width), F32)] + [sds((sub, width), BF16)] * (deep - 1),
        [VMEM] * 2,
        [keep, got],
        name="add_x",
    )
    p_got = [move(x, "col", 2 * k + 2) for k, x in enumerate(p_send)]
    steps = [n_col * 2**i for i in range(1, n_row.bit_length() - 1)]
    steps += [*(2**i for i in range(1, n_col.bit_length() - 1)), 1]
    for k in steps:
        w_mine, w_got = w_total, lax.ppermute(
            w_total, ("row", "col"), [(j, j ^ n_col ^ k) for j in range(n_row * n_col)]
        )
        if k != steps[-1]:
            w_total = add_w(w_mine, w_got)
        if k == steps[0]:
            q_keep, q_send = call(
                functools.partial(cut, n_row),
                [sds((n_row // 2, width, sub), F32)] * 2,
                [VMEM] * 2,
                [q_total, w_total],
                name="cut",
            )
            q_got = move(q_send, "row", 1)
    q_own, *q_out = call(
        add_pairs,
        [sds((width, sub), F32)] + [sds((width, sub), BF16)] * len(x_far),
        [VMEM] * 2,
        [q_keep, q_got],
        name="add_core",
    )
    q_in = [move(x, "row", 2 * k + 3) for k, x in enumerate(q_out)]
    (feature_grad,) = call(
        finish_grad,
        [sds((1, sub, width), BF16)],
        [VMEM] * (1 + len(q_in)),
        [q_own, *q_in],
        name="finish_grad",
    )
    w_total, p_total = call(
        add_last,
        [sds(w_mine.shape, F32), sds((sub, width), BF16)],
        [HBM] + [VMEM] * (3 + len(p_got)),
        [far(feature_grad), w_mine, w_got, p_own, *p_got[::-1]],
        name="add_last",
    )
    (weight_grad,) = call(
        finish_weight,
        [sds((width, width), F32)],
        [VMEM] * 2,
        [w_total, move(w_total, "row", 1)],
        name="finish_weight",
    )

    (out_rows,) = call(
        finish_out,
        [sds((1, sub, width), BF16)],
        [VMEM] * 2,
        [p_total, w_near],
        name="finish_out",
    )
    return out_rows, weight_grad, feature_grad


def solution(mesh):
    in_specs = (
        P("col", "row", None),
        P("row", "col", None, None, None),
        P("row", "col", None),
        P("row", "col", None),
        P("row", "col"),
        P(),
        P("row", "col", None),
    )
    out_specs = (P("row", "col", None), P(), P("col", "row", None))
    return jax.shard_map(local, mesh=mesh, in_specs=in_specs, out_specs=out_specs, check_vma=False)
```

```python
import functools
import math

import jax
import jax.numpy as jnp
from jax import lax
from jax.experimental import pallas as pl
from jax.experimental.pallas import tpu as pltpu
from jax.sharding import PartitionSpec as P

F32 = jnp.float32
BF16 = jnp.bfloat16
VMEM = pl.BlockSpec(memory_space=pltpu.VMEM)
SMEM = pl.BlockSpec(memory_space=pltpu.SMEM)
HBM = pl.BlockSpec(memory_space=pltpu.HBM)


def call(body, outs, ins, operands, scratch=(), flops=0, name=None):
    sizes = [math.prod(o.shape) * o.dtype.itemsize for o in outs]
    sizes += [math.prod(o.shape) * o.dtype.itemsize for o in operands]
    limit = sum(sizes) + sum(math.prod(s.shape) * 4 for s in scratch) + 2 * 1024 * 1024
    return pl.pallas_call(
        body,
        out_shape=outs,
        in_specs=ins,
        out_specs=[VMEM] * len(outs),
        scratch_shapes=scratch,
        compiler_params=pltpu.CompilerParams(vmem_limit_bytes=limit),
        cost_estimate=pl.CostEstimate(flops=flops, bytes_accessed=sum(sizes), transcendentals=0),
        name=name,
    )(*operands)


def sds(shape, dtype):
    return jax.ShapeDtypeStruct(shape, dtype)


def join(count, token_ref, side_ref, *refs):
    passed = (len(refs) - count - 1) // 2
    ins, out, copies = refs[: count + passed], refs[count + passed], refs[count + passed + 1 :]
    for k in range(count):
        out[count - 1 - k] = ins[k][...]
    for k, ref in enumerate(copies):
        ref[...] = ins[count + k][...]


def densify(live_ref, rows_hbm, cols_hbm, values_hbm, *refs):
    count = (len(refs) - 5) // 2
    tile_ref = refs[count]
    rows_ref, cols_ref, sems, few = refs[2 * count + 1 :]
    block = values_hbm.shape[3]
    pairs = ((rows_hbm, rows_ref), (cols_hbm, cols_ref))
    pairs += tuple(zip(refs[:count], refs[count + 1 : 2 * count + 1]))
    copies = [pltpu.make_async_copy(a, b, few.at[i]) for i, (a, b) in enumerate(pairs)]
    for one in copies:
        one.start()

    def clear(i, carry):
        tile_ref[pl.ds(i * block, block), :] = jnp.zeros((block, tile_ref.shape[1]), tile_ref.dtype)
        return carry

    lax.fori_loop(0, tile_ref.shape[0] // block, clear, 0)
    for one in copies[:2]:
        one.wait()
    live = live_ref[0, 0]

    def copy(s):
        r = pl.multiple_of(rows_ref[0, 0, s] * block, block)
        c = pl.multiple_of(cols_ref[0, 0, s] * block, block)
        return pltpu.make_async_copy(
            values_hbm.at[0, 0, s], tile_ref.at[pl.ds(r, block), pl.ds(c, block)], sems.at[s]
        )

    def start(s, carry):
        copy(s).start()
        return carry

    def wait(s, carry):
        copy(s).wait()
        return carry

    lax.fori_loop(0, live, start, 0)
    for one in copies[2:]:
        one.wait()
    lax.fori_loop(0, live, wait, 0)


def aggregate(n_row, n_col, tile_ref, *refs):
    parts = refs[:n_row]
    keep_ref, send_ref, whole = refs[n_row:]
    sub = parts[0].shape[0]
    row, col = lax.axis_index("row"), lax.axis_index("col")
    for k in range(n_row):
        whole[pl.ds(pl.multiple_of((row ^ k) * sub, sub), sub), :] = parts[k][...]
    for k in range(n_col):
        begin = pl.multiple_of((col ^ k) * sub, sub)
        part = jnp.dot(tile_ref[pl.ds(begin, sub), :], whole[...], preferred_element_type=F32)
        if k % 2:
            send_ref[k // 2] = part.astype(BF16)
        else:
            keep_ref[k // 2] = part


def own_half(rows):
    bits = (lax.axis_index("row"), lax.axis_index("col"))
    parity = 0
    for index, axis in zip(bits, ("row", "col")):
        for b in range(lax.axis_size(axis).bit_length() - 1):
            parity = parity ^ ((index >> b) & 1)
    mine = pl.multiple_of(parity * rows, rows)
    return pl.ds(mine, rows), pl.ds(pl.multiple_of(rows - mine, rows), rows)


def cotangent_of(refs, z):
    return (refs[1][refs[1].shape[0] - z] if z else refs[0][...]).T


def weight_term(n_col, scale, *refs):
    keep_ref, send_ref, token_ref, mine_ref, other_ref, whole = refs[4:]
    total = jnp.zeros(whole.shape, F32)
    for z in range(n_col // 2):
        for side in range(2):
            part = send_ref[z] if side else keep_ref[z].astype(BF16)
            cot = cotangent_of(refs[2 * side : 2 * side + 2], z)
            total += jnp.dot(cot, part, preferred_element_type=F32)
    whole[...] = total.T * scale
    mine, other = own_half(mine_ref.shape[0])
    mine_ref[...] = whole[mine, :]
    other_ref[...] = whole[other, :]


def finish_weight(mine_ref, other_ref, out_ref):
    mine, other = own_half(mine_ref.shape[0])
    out_ref[mine, :] = mine_ref[...]
    out_ref[other, :] = other_ref[...]


def feature_terms(n_col, side, own_ref, far_ref, tile_ref, weight_ref, *refs):
    total_ref, before_ref = refs[-1], refs[0] if side else None
    sub = own_ref.shape[0]
    col = lax.axis_index("col")
    weight = weight_ref[...]
    for z in range(n_col // 2):
        begin = pl.multiple_of((col ^ (2 * z + side)) * sub, sub)
        cot = cotangent_of((own_ref, far_ref), z)
        grad = jnp.dot(weight, cot, preferred_element_type=F32).astype(BF16)
        term = jnp.dot(grad, tile_ref[pl.ds(begin, sub), :], preferred_element_type=F32)
        if z > 0:
            total_ref[...] += term
        elif before_ref is not None:
            total_ref[...] = before_ref[...] + term
        else:
            total_ref[...] = term


def cut(n_row, total_ref, token_ref, q_keep, q_send):
    sub = q_keep.shape[2]
    row = lax.axis_index("row")
    for k in range(n_row):
        begin = pl.multiple_of((row ^ k) * sub, sub)
        piece = total_ref[:, pl.ds(begin, sub)]
        if (k + (k > 1)) % 2:
            q_send[k // 2] = piece
        else:
            q_keep[k // 2] = piece


def add_pairs(keep_ref, got_ref, own_ref, *send_refs):
    own_ref[...] = keep_ref[0] + got_ref[0].astype(F32)
    for k, ref in enumerate(send_refs):
        ref[...] = (keep_ref[k + 1] + got_ref[k + 1].astype(F32)).astype(BF16)


def add_tree(count, *refs):
    terms = [ref[...] for ref in refs[:count]]
    while len(terms) > 1:
        half = len(terms) // 2
        terms = [terms[k] + terms[half + k] for k in range(half)]
    refs[-1][...] = terms[0]


def add_last(after_ref, a_ref, b_ref, *refs):
    refs[-2][...] = a_ref[...] + b_ref[...]
    total = refs[0][...]
    for ref in refs[-3:0:-1]:
        total += ref[...].astype(F32)
    refs[-1][...] = total.astype(BF16)


def finish_out(total_ref, weight_ref, out_ref):
    out_ref[0] = jnp.dot(total_ref[...], weight_ref[...], preferred_element_type=F32).astype(BF16)


def finish_grad(own_ref, *refs):
    total = own_ref[...]
    for ref in refs[:-1]:
        total += ref[...].astype(F32)
    refs[-1][0] = total.T.astype(BF16)


def local(features, block_values, block_row, block_col, block_occupancy, weight, cotangent):
    n_row, n_col = lax.axis_size("row"), lax.axis_size("col")
    sub, width = features.shape[1:]
    slots, block = block_values.shape[2:4]
    rows, cols = n_col * sub, n_row * sub
    x_own, c_own = features[0], cotangent[0]

    def move(x, axis, k):
        n = lax.axis_size(axis)
        return lax.ppermute(x, axis, [(i, i ^ k) for i in range(n)])

    def far(x):
        return pltpu.with_memory_space_constraint(x, pltpu.HBM)

    deep = n_col // 2
    c_deep = [move(c_own, "col", 2 * k) for k in range(deep - 1, 0, -1)]
    x_far = [move(x_own, "row", k) for k in range(3, n_row, 2)]
    tile, c_near, w_near, x_near = call(
        densify,
        [
            sds((rows, cols), BF16),
            sds((sub, width), BF16),
            sds((width, width), BF16),
            sds((sub, width), BF16),
        ],
        [SMEM] + [HBM] * 6,
        [block_occupancy, *map(far, (block_row, block_col, block_values, c_own, weight, x_own))],
        [
            pltpu.SMEM(block_row.shape, jnp.int32),
            pltpu.SMEM(block_row.shape, jnp.int32),
            pltpu.SemaphoreType.DMA((slots,)),
            pltpu.SemaphoreType.DMA((5,)),
        ],
        name="densify",
    )
    c_side = move(c_own, "col", 1)
    c_far, *x_far = call(
        functools.partial(join, deep - 1),
        [sds((deep - 1, sub, width), BF16)] + [sds((sub, width), BF16)] * len(x_far),
        [VMEM] * (deep + 1 + len(x_far)),
        [w_near, c_side, *c_deep[::-1], *x_far],
        name="join",
    )
    c_side = [c_side, move(c_far, "col", 1)]
    x_parts = [x_near, move(x_own, "row", 1)]
    for x in x_far:
        x_parts += [move(x, "row", 1), x]
    keep, send = call(
        functools.partial(aggregate, n_row, n_col),
        [sds((deep, sub, width), F32), sds((deep, sub, width), BF16)],
        [VMEM] * (n_row + 1),
        [tile, *x_parts],
        [pltpu.VMEM((cols, width), BF16)],
        flops=2 * rows * cols * width,
        name="aggregate",
    )
    c_own_side = [c_near, c_far]
    (q_near,) = call(
        functools.partial(feature_terms, n_col, 0),
        [sds((width, cols), F32)],
        [VMEM] * 4,
        [*c_own_side, tile, w_near],
        flops=rows * cols * width,
        name="feature_near",
    )
    got = move(send, "col", 1)
    w_part, w_other = call(
        functools.partial(weight_term, n_col, 1.0 / math.sqrt(n_row * rows)),
        [sds((width // 2, width), F32)] * 2,
        [VMEM] * 7,
        [*c_own_side, *c_side, keep, send, q_near],
        [pltpu.VMEM((width, width), F32)],
        flops=2 * rows * width * width,
        name="weight_term",
    )
    w_got = move(w_other, "row", 1)
    (w_total,) = call(
        functools.partial(add_tree, 2),
        [sds(w_part.shape, F32)],
        [VMEM] * 2,
        [w_part, w_got],
        name="add_w",
    )
    (q_total,) = call(
        functools.partial(feature_terms, n_col, 1),
        [sds((width, cols), F32)],
        [VMEM] * 6,
        [*c_side, tile, w_near, q_near, w_total],
        flops=rows * cols * width,
        name="feature_side",
    )
    p_own, *p_send = call(
        add_pairs,
        [sds((sub, width), F32)] + [sds((sub, width), BF16)] * (deep - 1),
        [VMEM] * 2,
        [keep, got],
        name="add_x",
    )
    p_got = [move(x, "col", 2 * k + 2) for k, x in enumerate(p_send)]
    def turn(x, mask):
        mask ^= n_col * (mask.bit_count() % 2)
        return lax.ppermute(x, ("row", "col"), [(j, j ^ mask) for j in range(n_row * n_col)])

    def add_w(mine, *got, after=()):
        (total,) = call(
            functools.partial(add_tree, 1 + len(got)),
            [sds(mine.shape, F32)],
            [VMEM] * (1 + len(got) + len(after)),
            [mine, *got, *after],
            name="add_w",
        )
        return total

    for i in range(1, n_row.bit_length() - 1):
        w_total = add_w(w_total, turn(w_total, n_col * 2**i))
    q_keep, q_send = call(
        functools.partial(cut, n_row),
        [sds((n_row // 2, width, sub), F32)] * 2,
        [VMEM] * 2,
        [q_total, w_total],
        name="cut",
    )
    q_got = move(q_send, "row", 1)
    w_total = add_w(w_total, *[turn(w_total, 2 * k) for k in range(1, deep)])
    w_mine, w_got = w_total, turn(w_total, 1)
    q_own, *q_out = call(
        add_pairs,
        [sds((width, sub), F32)] + [sds((width, sub), BF16)] * len(x_far),
        [VMEM] * 2,
        [q_keep, q_got],
        name="add_core",
    )
    q_in = [move(x, "row", 2 * k + 3) for k, x in enumerate(q_out)]
    (feature_grad,) = call(
        finish_grad,
        [sds((1, sub, width), BF16)],
        [VMEM] * (1 + len(q_in)),
        [q_own, *q_in],
        name="finish_grad",
    )
    w_total, p_total = call(
        add_last,
        [sds(w_mine.shape, F32), sds((sub, width), BF16)],
        [HBM] + [VMEM] * (3 + len(p_got)),
        [far(feature_grad), w_mine, w_got, p_own, *p_got[::-1]],
        name="add_last",
    )
    (weight_grad,) = call(
        finish_weight,
        [sds((width, width), F32)],
        [VMEM] * 2,
        [w_total, move(w_total, "row", 1)],
        name="finish_weight",
    )

    (out_rows,) = call(
        finish_out,
        [sds((1, sub, width), BF16)],
        [VMEM] * 2,
        [p_total, w_near],
        name="finish_out",
    )
    return out_rows, weight_grad, feature_grad


def solution(mesh):
    in_specs = (
        P("col", "row", None),
        P("row", "col", None, None, None),
        P("row", "col", None),
        P("row", "col", None),
        P("row", "col"),
        P(),
        P("row", "col", None),
    )
    out_specs = (P("row", "col", None), P(), P("col", "row", None))
    return jax.shard_map(local, mesh=mesh, in_specs=in_specs, out_specs=out_specs, check_vma=False)
```

```python
import functools
import math

import jax
import jax.numpy as jnp
from jax import lax
from jax.experimental import pallas as pl
from jax.experimental.pallas import tpu as pltpu
from jax.sharding import PartitionSpec as P

F32 = jnp.float32
BF16 = jnp.bfloat16
VMEM = pl.BlockSpec(memory_space=pltpu.VMEM)
SMEM = pl.BlockSpec(memory_space=pltpu.SMEM)
HBM = pl.BlockSpec(memory_space=pltpu.HBM)


def call(body, outs, ins, operands, scratch=(), flops=0, name=None):
    sizes = [math.prod(o.shape) * o.dtype.itemsize for o in outs]
    sizes += [math.prod(o.shape) * o.dtype.itemsize for o in operands]
    limit = sum(sizes) + sum(math.prod(s.shape) * 4 for s in scratch) + 2 * 1024 * 1024
    return pl.pallas_call(
        body,
        out_shape=outs,
        in_specs=ins,
        out_specs=[VMEM] * len(outs),
        scratch_shapes=scratch,
        compiler_params=pltpu.CompilerParams(vmem_limit_bytes=limit),
        cost_estimate=pl.CostEstimate(flops=flops, bytes_accessed=sum(sizes), transcendentals=0),
        name=name,
    )(*operands)


def sds(shape, dtype):
    return jax.ShapeDtypeStruct(shape, dtype)


def join(order, *refs):
    ins = dict(zip(order, refs))
    out, copies = refs[len(order)], refs[len(order) + 1 :]
    for k in range(out.shape[0]):
        out[k] = ins["c", k][...]
    for k, ref in enumerate(copies):
        ref[...] = ins["x", k][...]


def densify(live_ref, rows_hbm, cols_hbm, values_hbm, *refs):
    count = (len(refs) - 5) // 2
    tile_ref = refs[count]
    rows_ref, cols_ref, sems, few = refs[2 * count + 1 :]
    block = values_hbm.shape[3]
    pairs = ((rows_hbm, rows_ref), (cols_hbm, cols_ref))
    pairs += tuple(zip(refs[:count], refs[count + 1 : 2 * count + 1]))
    copies = [pltpu.make_async_copy(a, b, few.at[i]) for i, (a, b) in enumerate(pairs)]
    for one in copies:
        one.start()

    def clear(i, carry):
        tile_ref[pl.ds(i * block, block), :] = jnp.zeros((block, tile_ref.shape[1]), tile_ref.dtype)
        return carry

    lax.fori_loop(0, tile_ref.shape[0] // block, clear, 0)
    for one in copies[:2]:
        one.wait()
    live = live_ref[0, 0]

    def copy(s):
        r = pl.multiple_of(rows_ref[0, 0, s] * block, block)
        c = pl.multiple_of(cols_ref[0, 0, s] * block, block)
        return pltpu.make_async_copy(
            values_hbm.at[0, 0, s], tile_ref.at[pl.ds(r, block), pl.ds(c, block)], sems.at[s]
        )

    def start(s, carry):
        copy(s).start()
        return carry

    def wait(s, carry):
        copy(s).wait()
        return carry

    lax.fori_loop(0, live, start, 0)
    for one in copies[2:]:
        one.wait()
    lax.fori_loop(0, live, wait, 0)


def aggregate(n_row, n_col, tile_ref, *refs):
    parts = refs[:n_row]
    keep_ref, *send_refs, whole = refs[n_row:]
    sub = parts[0].shape[0]
    row, col = lax.axis_index("row"), lax.axis_index("col")
    for k in range(n_row):
        whole[pl.ds(pl.multiple_of((row ^ k) * sub, sub), sub), :] = parts[k][...]
    for k in range(n_col):
        begin = pl.multiple_of((col ^ k) * sub, sub)
        part = jnp.dot(tile_ref[pl.ds(begin, sub), :], whole[...], preferred_element_type=F32)
        if k < 2:
            keep_ref[k] = part
        else:
            send_refs[k // 2 - 1][k % 2] = part.astype(BF16)


def own_half(rows):
    bits = (lax.axis_index("row"), lax.axis_index("col"))
    parity = 0
    for index, axis in zip(bits, ("row", "col")):
        for b in range(lax.axis_size(axis).bit_length() - 1):
            parity = parity ^ ((index >> b) & 1)
    mine = pl.multiple_of(parity * rows, rows)
    return pl.ds(mine, rows), pl.ds(pl.multiple_of(rows - mine, rows), rows)


def weight_term(n_col, scale, *refs):
    parts = refs[2 : 2 + n_col // 2]
    mine_ref, other_ref, whole = refs[2 + n_col // 2 :]
    total = jnp.zeros(whole.shape, F32)
    for z, part in enumerate(parts):
        for side in range(2):
            term = part[side].astype(BF16)
            total += jnp.dot(refs[side][z].T, term, preferred_element_type=F32)
    whole[...] = total.T * scale
    mine, other = own_half(mine_ref.shape[0])
    mine_ref[...] = whole[mine, :]
    other_ref[...] = whole[other, :]


def finish_weight(mine_ref, other_ref, after_ref, out_ref):
    mine, other = own_half(mine_ref.shape[0])
    out_ref[mine, :] = mine_ref[...]
    out_ref[other, :] = other_ref[...]


def feature_terms(side, cot_ref, tile_ref, weight_ref, *refs):
    total_ref, before_ref = refs[-1], refs[0] if side else None
    deep, sub = cot_ref.shape[:2]
    col = lax.axis_index("col")
    weight = weight_ref[...]
    for z in range(deep):
        begin = pl.multiple_of((col ^ (2 * z + side)) * sub, sub)
        grad = jnp.dot(weight, cot_ref[z].T, preferred_element_type=F32).astype(BF16)
        term = jnp.dot(grad, tile_ref[pl.ds(begin, sub), :], preferred_element_type=F32)
        if z > 0:
            total_ref[...] += term
        elif before_ref is not None:
            total_ref[...] = before_ref[...] + term
        else:
            total_ref[...] = term


def cut(n_row, total_ref, token_ref, after_ref, q_keep, q_send):
    sub = q_keep.shape[2]
    row = lax.axis_index("row")
    for k in range(n_row):
        begin = pl.multiple_of((row ^ k) * sub, sub)
        piece = total_ref[:, pl.ds(begin, sub)]
        if (k + (k > 1)) % 2:
            q_send[k // 2] = piece
        else:
            q_keep[k // 2] = piece


def add_deep(keep_ref, *refs):
    own, other = keep_ref[0], keep_ref[1]
    for ref in refs[:-2]:
        own += ref[0].astype(F32)
        other += ref[1].astype(F32)
    refs[-2][...] = own
    refs[-1][...] = other.astype(BF16)


def add_pairs(keep_ref, got_ref, own_ref, *send_refs):
    own_ref[...] = keep_ref[0] + got_ref[0].astype(F32)
    for k, ref in enumerate(send_refs):
        ref[...] = (keep_ref[k + 1] + got_ref[k + 1].astype(F32)).astype(BF16)


def add_tree(count, *refs):
    terms = [ref[...] for ref in (refs[0], *refs[count - 1 : 0 : -1])]
    while len(terms) > 1:
        half = len(terms) // 2
        terms = [terms[k] + terms[half + k] for k in range(half)]
    refs[-1][...] = terms[0]


def add_last(count, *refs):
    add_tree(count, *refs[:count], refs[-2])
    refs[-1][...] = (refs[count][...] + refs[count + 1][...].astype(F32)).astype(BF16)


def finish(total_ref, weight_ref, own_ref, *refs):
    out_ref, grad_ref = refs[-2:]
    out_ref[0] = jnp.dot(total_ref[...], weight_ref[...], preferred_element_type=F32).astype(BF16)
    total = own_ref[...]
    for ref in refs[:-2]:
        total += ref[...].astype(F32)
    grad_ref[0] = total.T.astype(BF16)


def local(features, block_values, block_row, block_col, block_occupancy, weight, cotangent):
    n_row, n_col = lax.axis_size("row"), lax.axis_size("col")
    sub, width = features.shape[1:]
    slots, block = block_values.shape[2:4]
    rows, cols = n_col * sub, n_row * sub
    x_own, c_own = features[0], cotangent[0]

    def move(x, axis, k):
        n = lax.axis_size(axis)
        return lax.ppermute(x, axis, [(i, i ^ k) for i in range(n)])

    def far(x):
        return pltpu.with_memory_space_constraint(x, pltpu.HBM)

    deep = n_col // 2
    c_deep = [move(c_own, "col", 2 * k) for k in range(deep - 1, 0, -1)]
    x_far = [move(x_own, "row", k) for k in range(3, n_row, 2)]
    tile, c_near, w_near, x_near = call(
        densify,
        [
            sds((rows, cols), BF16),
            sds((sub, width), BF16),
            sds((width, width), BF16),
            sds((sub, width), BF16),
        ],
        [SMEM] + [HBM] * 6,
        [block_occupancy, *map(far, (block_row, block_col, block_values, c_own, weight, x_own))],
        [
            pltpu.SMEM(block_row.shape, jnp.int32),
            pltpu.SMEM(block_row.shape, jnp.int32),
            pltpu.SemaphoreType.DMA((slots,)),
            pltpu.SemaphoreType.DMA((5,)),
        ],
        name="densify",
    )
    moved = {("c", k): x for k, x in enumerate([c_near, *c_deep[::-1]])}
    moved |= {("x", k): x for k, x in enumerate(x_far)}
    order = list(moved)[:1] + list(moved)[deep - 1 : 0 : -1] + list(moved)[deep:]
    c_deep, *x_far = call(
        functools.partial(join, order),
        [sds((deep, sub, width), BF16)] + [sds((sub, width), BF16)] * len(x_far),
        [VMEM] * len(order),
        [moved[key] for key in order],
        name="join",
    )
    c_side = move(c_deep, "col", 1)
    x_parts = [x_near, move(x_own, "row", 1)]
    for x in x_far:
        x_parts += [move(x, "row", 1), x]
    keep, *send = call(
        functools.partial(aggregate, n_row, n_col),
        [sds((2, sub, width), F32)] + [sds((2, sub, width), BF16)] * (deep - 1),
        [VMEM] * (n_row + 1),
        [tile, *x_parts],
        [pltpu.VMEM((cols, width), BF16)],
        flops=2 * rows * cols * width,
        name="aggregate",
    )
    got = [move(send[k], "col", 2 * k + 2) for k in range(deep - 2, -1, -1)]
    w_part, w_other = call(
        functools.partial(weight_term, n_col, 1.0 / math.sqrt(n_row * rows)),
        [sds((width // 2, width), F32)] * 2,
        [VMEM] * (2 + deep),
        [c_deep, c_side, keep, *send],
        [pltpu.VMEM((width, width), F32)],
        flops=2 * rows * width * width,
        name="weight_term",
    )
    w_got = move(w_other, "row", 1)
    (w_total,) = call(
        functools.partial(add_tree, 2),
        [sds(w_part.shape, F32)],
        [VMEM] * 2,
        [w_part, w_got],
        name="add_w",
    )
    (q_near,) = call(
        functools.partial(feature_terms, 0),
        [sds((width, cols), F32)],
        [VMEM] * 4,
        [c_deep, tile, w_near, w_total],
        flops=rows * cols * width,
        name="feature_near",
    )
    (q_total,) = call(
        functools.partial(feature_terms, 1),
        [sds((width, cols), F32)],
        [VMEM] * 5,
        [c_side, tile, w_near, q_near, w_total],
        flops=rows * cols * width,
        name="feature_side",
    )
    p_own, p_send = call(
        add_deep,
        [sds((sub, width), F32), sds((sub, width), BF16)],
        [VMEM] * deep,
        [keep, *got],
        name="add_deep",
    )
    p_got = [move(p_send, "col", 1)]
    def turn(x, mask):
        mask ^= n_col * (mask.bit_count() % 2)
        return lax.ppermute(x, ("row", "col"), [(j, j ^ mask) for j in range(n_row * n_col)])

    def add_w(mine, *got, after=()):
        (total,) = call(
            functools.partial(add_tree, 1 + len(got)),
            [sds(mine.shape, F32)],
            [VMEM] * (1 + len(got) + len(after)),
            [mine, *got, *after],
            name="add_w",
        )
        return total

    for i in range(1, n_row.bit_length() - 1):
        w_total = add_w(w_total, turn(w_total, n_col * 2**i), after=[q_total])
    w_total = add_w(w_total, turn(w_total, 1))
    q_keep, q_send = call(
        functools.partial(cut, n_row),
        [sds((n_row // 2, width, sub), F32)] * 2,
        [VMEM] * 3,
        [q_total, w_total, p_own],
        name="cut",
    )
    q_got = move(q_send, "row", 1)
    w_got = [turn(w_total, 2 * k) for k in range(deep - 1, 0, -1)]
    q_own, *q_out = call(
        add_pairs,
        [sds((width, sub), F32)] + [sds((width, sub), BF16)] * len(x_far),
        [VMEM] * 2,
        [q_keep, q_got],
        name="add_core",
    )
    q_in = [move(x, "row", 2 * k + 3) for k, x in enumerate(q_out)]
    w_total, p_total = call(
        functools.partial(add_last, deep),
        [sds(w_total.shape, F32), sds((sub, width), BF16)],
        [VMEM] * (deep + 2),
        [w_total, *w_got, p_own, *p_got],
        name="add_last",
    )

    w_mate = move(w_total, "row", 1)
    out_rows, feature_grad = call(
        finish,
        [sds((1, sub, width), BF16)] * 2,
        [VMEM] * (3 + len(q_in)),
        [p_total, w_near, q_own, *q_in],
        name="finish",
    )
    (weight_grad,) = call(
        finish_weight,
        [sds((width, width), F32)],
        [VMEM] * 2 + [HBM],
        [w_total, w_mate, far(out_rows)],
        name="finish_weight",
    )
    return out_rows, weight_grad, feature_grad


def solution(mesh):
    in_specs = (
        P("col", "row", None),
        P("row", "col", None, None, None),
        P("row", "col", None),
        P("row", "col", None),
        P("row", "col"),
        P(),
        P("row", "col", None),
    )
    out_specs = (P("row", "col", None), P(), P("col", "row", None))
    return jax.shard_map(local, mesh=mesh, in_specs=in_specs, out_specs=out_specs, check_vma=False)
```

```python
import functools
import math

import jax
import jax.numpy as jnp
from jax import lax
from jax.experimental import pallas as pl
from jax.experimental.pallas import tpu as pltpu
from jax.sharding import PartitionSpec as P

F32 = jnp.float32
BF16 = jnp.bfloat16
VMEM = pl.BlockSpec(memory_space=pltpu.VMEM)
SMEM = pl.BlockSpec(memory_space=pltpu.SMEM)
HBM = pl.BlockSpec(memory_space=pltpu.HBM)


def call(body, outs, ins, operands, scratch=(), flops=0, name=None):
    sizes = [math.prod(o.shape) * o.dtype.itemsize for o in outs]
    sizes += [math.prod(o.shape) * o.dtype.itemsize for o in operands]
    limit = sum(sizes) + sum(math.prod(s.shape) * 4 for s in scratch) + 2 * 1024 * 1024
    return pl.pallas_call(
        body,
        out_shape=outs,
        in_specs=ins,
        out_specs=[VMEM] * len(outs),
        scratch_shapes=scratch,
        compiler_params=pltpu.CompilerParams(vmem_limit_bytes=limit),
        cost_estimate=pl.CostEstimate(flops=flops, bytes_accessed=sum(sizes), transcendentals=0),
        name=name,
    )(*operands)


def sds(shape, dtype):
    return jax.ShapeDtypeStruct(shape, dtype)


def join(order, *refs):
    ins = dict(zip(order, refs))
    out, copies = refs[len(order)], refs[len(order) + 1 :]
    for k in range(out.shape[0]):
        out[k] = ins["c", k][...]
    for k, ref in enumerate(copies):
        ref[...] = ins["x", k][...]


def densify(live_ref, rows_hbm, cols_hbm, values_hbm, *refs):
    count = (len(refs) - 5) // 2
    tile_ref = refs[count]
    rows_ref, cols_ref, sems, few = refs[2 * count + 1 :]
    block = values_hbm.shape[3]
    pairs = ((rows_hbm, rows_ref), (cols_hbm, cols_ref))
    pairs += tuple(zip(refs[:count], refs[count + 1 : 2 * count + 1]))
    copies = [pltpu.make_async_copy(a, b, few.at[i]) for i, (a, b) in enumerate(pairs)]
    for one in copies:
        one.start()

    def clear(i, carry):
        tile_ref[pl.ds(i * block, block), :] = jnp.zeros((block, tile_ref.shape[1]), tile_ref.dtype)
        return carry

    lax.fori_loop(0, tile_ref.shape[0] // block, clear, 0)
    for one in copies[:2]:
        one.wait()
    live = live_ref[0, 0]

    def copy(s):
        r = pl.multiple_of(rows_ref[0, 0, s] * block, block)
        c = pl.multiple_of(cols_ref[0, 0, s] * block, block)
        return pltpu.make_async_copy(
            values_hbm.at[0, 0, s], tile_ref.at[pl.ds(r, block), pl.ds(c, block)], sems.at[s]
        )

    def start(s, carry):
        copy(s).start()
        return carry

    def wait(s, carry):
        copy(s).wait()
        return carry

    lax.fori_loop(0, live, start, 0)
    for one in copies[2:]:
        one.wait()
    lax.fori_loop(0, live, wait, 0)


def products(order, col_block, tile_ref, parts):
    sub = parts[0].shape[0]
    row = lax.axis_index("row")
    begin = pl.multiple_of((lax.axis_index("col") ^ col_block) * sub, sub)
    total = None
    for k, part in zip(order, parts):
        across = pl.multiple_of((row ^ k) * sub, sub)
        block = tile_ref[pl.ds(begin, sub), pl.ds(across, sub)]
        term = jnp.dot(block, part[...], preferred_element_type=F32)
        total = term if total is None else total + term
    return total


def aggregate_ready(order, n_col, tile_ref, *refs):
    for k in range(n_col):
        refs[-1][k] = products(order, k, tile_ref, refs[:-1])


def aggregate(order, n_col, tile_ref, before_ref, *refs):
    parts = refs[: len(order)]
    keep_ref, *send_refs = refs[len(order) :]
    for k in range(n_col):
        part = before_ref[k] + products(order, k, tile_ref, parts)
        if k < 2:
            keep_ref[k] = part
        else:
            send_refs[k // 2 - 1][k % 2] = part.astype(BF16)


def own_half(rows):
    bits = (lax.axis_index("row"), lax.axis_index("col"))
    parity = 0
    for index, axis in zip(bits, ("row", "col")):
        for b in range(lax.axis_size(axis).bit_length() - 1):
            parity = parity ^ ((index >> b) & 1)
    mine = pl.multiple_of(parity * rows, rows)
    return pl.ds(mine, rows), pl.ds(pl.multiple_of(rows - mine, rows), rows)


def weight_term(n_col, scale, *refs):
    parts = refs[2 : 2 + n_col // 2]
    mine_ref, other_ref, whole = refs[2 + n_col // 2 :]
    total = jnp.zeros(whole.shape, F32)
    for z, part in enumerate(parts):
        for side in range(2):
            term = part[side].astype(BF16)
            total += jnp.dot(refs[side][z].T, term, preferred_element_type=F32)
    whole[...] = total.T * scale
    mine, other = own_half(mine_ref.shape[0])
    mine_ref[...] = whole[mine, :]
    other_ref[...] = whole[other, :]


def finish_weight(mine_ref, other_ref, after_ref, out_ref):
    mine, other = own_half(mine_ref.shape[0])
    out_ref[mine, :] = mine_ref[...]
    out_ref[other, :] = other_ref[...]


def feature_terms(side, cot_ref, tile_ref, weight_ref, *refs):
    total_ref, before_ref = refs[-1], refs[0] if side else None
    deep, sub = cot_ref.shape[:2]
    col = lax.axis_index("col")
    weight = weight_ref[...]
    for z in range(deep):
        begin = pl.multiple_of((col ^ (2 * z + side)) * sub, sub)
        grad = jnp.dot(weight, cot_ref[z].T, preferred_element_type=F32).astype(BF16)
        term = jnp.dot(grad, tile_ref[pl.ds(begin, sub), :], preferred_element_type=F32)
        if z > 0:
            total_ref[...] += term
        elif before_ref is not None:
            total_ref[...] = before_ref[...] + term
        else:
            total_ref[...] = term


def cut(n_row, total_ref, token_ref, after_ref, q_keep, q_send):
    sub = q_keep.shape[2]
    row = lax.axis_index("row")
    for k in range(n_row):
        begin = pl.multiple_of((row ^ k) * sub, sub)
        piece = total_ref[:, pl.ds(begin, sub)]
        if (k + (k > 1)) % 2:
            q_send[k // 2] = piece
        else:
            q_keep[k // 2] = piece


def add_deep(keep_ref, *refs):
    own, other = keep_ref[0], keep_ref[1]
    for ref in refs[:-2]:
        own += ref[0].astype(F32)
        other += ref[1].astype(F32)
    refs[-2][...] = own
    refs[-1][...] = other.astype(BF16)


def add_pairs(keep_ref, got_ref, own_ref, *send_refs):
    own_ref[...] = keep_ref[0] + got_ref[0].astype(F32)
    for k, ref in enumerate(send_refs):
        ref[...] = (keep_ref[k + 1] + got_ref[k + 1].astype(F32)).astype(BF16)


def add_tree(count, *refs):
    terms = [ref[...] for ref in (refs[0], *refs[count - 1 : 0 : -1])]
    while len(terms) > 1:
        half = len(terms) // 2
        terms = [terms[k] + terms[half + k] for k in range(half)]
    refs[-1][...] = terms[0]


def add_last(count, *refs):
    add_tree(count, *refs[:count], refs[-2])
    refs[-1][...] = (refs[count][...] + refs[count + 1][...].astype(F32)).astype(BF16)


def finish(total_ref, weight_ref, own_ref, *refs):
    out_ref, grad_ref = refs[-2:]
    out_ref[0] = jnp.dot(total_ref[...], weight_ref[...], preferred_element_type=F32).astype(BF16)
    total = own_ref[...]
    for ref in refs[:-2]:
        total += ref[...].astype(F32)
    grad_ref[0] = total.T.astype(BF16)


def local(features, block_values, block_row, block_col, block_occupancy, weight, cotangent):
    n_row, n_col = lax.axis_size("row"), lax.axis_size("col")
    sub, width = features.shape[1:]
    slots, block = block_values.shape[2:4]
    rows, cols = n_col * sub, n_row * sub
    x_own, c_own = features[0], cotangent[0]

    def move(x, axis, k):
        n = lax.axis_size(axis)
        return lax.ppermute(x, axis, [(i, i ^ k) for i in range(n)])

    def far(x):
        return pltpu.with_memory_space_constraint(x, pltpu.HBM)

    deep = n_col // 2
    c_deep = [move(c_own, "col", 2 * k) for k in range(deep - 1, 0, -1)]
    x_far = [move(x_own, "row", k) for k in range(3, n_row, 2)]
    tile, c_near, w_near, x_near = call(
        densify,
        [
            sds((rows, cols), BF16),
            sds((sub, width), BF16),
            sds((width, width), BF16),
            sds((sub, width), BF16),
        ],
        [SMEM] + [HBM] * 6,
        [block_occupancy, *map(far, (block_row, block_col, block_values, c_own, weight, x_own))],
        [
            pltpu.SMEM(block_row.shape, jnp.int32),
            pltpu.SMEM(block_row.shape, jnp.int32),
            pltpu.SemaphoreType.DMA((slots,)),
            pltpu.SemaphoreType.DMA((5,)),
        ],
        name="densify",
    )
    moved = {("c", k): x for k, x in enumerate([c_near, *c_deep[::-1]])}
    moved |= {("x", k): x for k, x in enumerate(x_far)}
    order = list(moved)[:1] + list(moved)[deep - 1 : 0 : -1] + list(moved)[deep:]
    c_deep, *x_far = call(
        functools.partial(join, order),
        [sds((deep, sub, width), BF16)] + [sds((sub, width), BF16)] * len(x_far),
        [VMEM] * len(order),
        [moved[key] for key in order],
        name="join",
    )
    c_side = move(c_deep, "col", 1)
    x_parts = [x_near, move(x_own, "row", 1)]
    for x in x_far:
        x_parts += [move(x, "row", 1), x]
    ready = [0, *range(3, n_row, 2)]
    waited = [1, *range(2, n_row, 2)]
    (p_ready,) = call(
        functools.partial(aggregate_ready, ready, n_col),
        [sds((n_col, sub, width), F32)],
        [VMEM] * (1 + len(ready)),
        [tile, *(x_parts[k] for k in ready)],
        flops=rows * cols * width,
        name="aggregate_ready",
    )
    keep, *send = call(
        functools.partial(aggregate, waited, n_col),
        [sds((2, sub, width), F32)] + [sds((2, sub, width), BF16)] * (deep - 1),
        [VMEM] * (2 + len(waited)),
        [tile, p_ready, *(x_parts[k] for k in waited)],
        flops=rows * cols * width,
        name="aggregate",
    )
    got = [move(send[k], "col", 2 * k + 2) for k in range(deep - 2, -1, -1)]
    w_part, w_other = call(
        functools.partial(weight_term, n_col, 1.0 / math.sqrt(n_row * rows)),
        [sds((width // 2, width), F32)] * 2,
        [VMEM] * (2 + deep),
        [c_deep, c_side, keep, *send],
        [pltpu.VMEM((width, width), F32)],
        flops=2 * rows * width * width,
        name="weight_term",
    )
    w_got = move(w_other, "row", 1)
    (w_total,) = call(
        functools.partial(add_tree, 2),
        [sds(w_part.shape, F32)],
        [VMEM] * 2,
        [w_part, w_got],
        name="add_w",
    )
    (q_near,) = call(
        functools.partial(feature_terms, 0),
        [sds((width, cols), F32)],
        [VMEM] * 4,
        [c_deep, tile, w_near, w_total],
        flops=rows * cols * width,
        name="feature_near",
    )
    (q_total,) = call(
        functools.partial(feature_terms, 1),
        [sds((width, cols), F32)],
        [VMEM] * 5,
        [c_side, tile, w_near, q_near, w_total],
        flops=rows * cols * width,
        name="feature_side",
    )
    p_own, p_send = call(
        add_deep,
        [sds((sub, width), F32), sds((sub, width), BF16)],
        [VMEM] * deep,
        [keep, *got],
        name="add_deep",
    )
    p_got = [move(p_send, "col", 1)]
    def turn(x, mask):
        mask ^= n_col * (mask.bit_count() % 2)
        return lax.ppermute(x, ("row", "col"), [(j, j ^ mask) for j in range(n_row * n_col)])

    def add_w(mine, *got, after=()):
        (total,) = call(
            functools.partial(add_tree, 1 + len(got)),
            [sds(mine.shape, F32)],
            [VMEM] * (1 + len(got) + len(after)),
            [mine, *got, *after],
            name="add_w",
        )
        return total

    for i in range(1, n_row.bit_length() - 1):
        w_total = add_w(w_total, turn(w_total, n_col * 2**i), after=[q_total])
    w_total = add_w(w_total, turn(w_total, 1))
    q_keep, q_send = call(
        functools.partial(cut, n_row),
        [sds((n_row // 2, width, sub), F32)] * 2,
        [VMEM] * 3,
        [q_total, w_total, p_own],
        name="cut",
    )
    q_got = move(q_send, "row", 1)
    w_got = [turn(w_total, 2 * k) for k in range(deep - 1, 0, -1)]
    q_own, *q_out = call(
        add_pairs,
        [sds((width, sub), F32)] + [sds((width, sub), BF16)] * len(x_far),
        [VMEM] * 2,
        [q_keep, q_got],
        name="add_core",
    )
    q_in = [move(x, "row", 2 * k + 3) for k, x in enumerate(q_out)]
    w_total, p_total = call(
        functools.partial(add_last, deep),
        [sds(w_total.shape, F32), sds((sub, width), BF16)],
        [VMEM] * (deep + 2),
        [w_total, *w_got, p_own, *p_got],
        name="add_last",
    )

    w_mate = move(w_total, "row", 1)
    out_rows, feature_grad = call(
        finish,
        [sds((1, sub, width), BF16)] * 2,
        [VMEM] * (3 + len(q_in)),
        [p_total, w_near, q_own, *q_in],
        name="finish",
    )
    (weight_grad,) = call(
        finish_weight,
        [sds((width, width), F32)],
        [VMEM] * 2 + [HBM],
        [w_total, w_mate, far(out_rows)],
        name="finish_weight",
    )
    return out_rows, weight_grad, feature_grad


def solution(mesh):
    in_specs = (
        P("col", "row", None),
        P("row", "col", None, None, None),
        P("row", "col", None),
        P("row", "col", None),
        P("row", "col"),
        P(),
        P("row", "col", None),
    )
    out_specs = (P("row", "col", None), P(), P("col", "row", None))
    return jax.shard_map(local, mesh=mesh, in_specs=in_specs, out_specs=out_specs, check_vma=False)
```

```python
import functools
import math

import jax
import jax.numpy as jnp
from jax import lax
from jax.experimental import pallas as pl
from jax.experimental.pallas import tpu as pltpu
from jax.sharding import PartitionSpec as P

F32 = jnp.float32
BF16 = jnp.bfloat16
VMEM = pl.BlockSpec(memory_space=pltpu.VMEM)
SMEM = pl.BlockSpec(memory_space=pltpu.SMEM)
HBM = pl.BlockSpec(memory_space=pltpu.HBM)


def call(body, outs, ins, operands, scratch=(), flops=0, name=None):
    sizes = [math.prod(o.shape) * o.dtype.itemsize for o in outs]
    sizes += [math.prod(o.shape) * o.dtype.itemsize for o in operands]
    limit = sum(sizes) + sum(math.prod(s.shape) * 4 for s in scratch) + 2 * 1024 * 1024
    return pl.pallas_call(
        body,
        out_shape=outs,
        in_specs=ins,
        out_specs=[VMEM] * len(outs),
        scratch_shapes=scratch,
        compiler_params=pltpu.CompilerParams(vmem_limit_bytes=limit),
        cost_estimate=pl.CostEstimate(flops=flops, bytes_accessed=sum(sizes), transcendentals=0),
        name=name,
    )(*operands)


def sds(shape, dtype):
    return jax.ShapeDtypeStruct(shape, dtype)


def join(order, *refs):
    ins = dict(zip(order, refs))
    out, copies = refs[len(order)], refs[len(order) + 1 :]
    for k in range(out.shape[0]):
        out[k] = ins["c", k][...]
    for k, ref in enumerate(copies):
        ref[...] = ins["x", k][...]


def densify(live_ref, rows_hbm, cols_hbm, values_hbm, *refs):
    count = (len(refs) - 5) // 2
    tile_ref = refs[count]
    rows_ref, cols_ref, sems, few = refs[2 * count + 1 :]
    block = values_hbm.shape[3]
    pairs = ((rows_hbm, rows_ref), (cols_hbm, cols_ref))
    pairs += tuple(zip(refs[:count], refs[count + 1 : 2 * count + 1]))
    copies = [pltpu.make_async_copy(a, b, few.at[i]) for i, (a, b) in enumerate(pairs)]
    for one in copies:
        one.start()

    def clear(i, carry):
        tile_ref[pl.ds(i * block, block), :] = jnp.zeros((block, tile_ref.shape[1]), tile_ref.dtype)
        return carry

    lax.fori_loop(0, tile_ref.shape[0] // block, clear, 0)
    for one in copies[:2]:
        one.wait()
    live = live_ref[0, 0]

    def copy(s):
        r = pl.multiple_of(rows_ref[0, 0, s] * block, block)
        c = pl.multiple_of(cols_ref[0, 0, s] * block, block)
        return pltpu.make_async_copy(
            values_hbm.at[0, 0, s], tile_ref.at[pl.ds(r, block), pl.ds(c, block)], sems.at[s]
        )

    def start(s, carry):
        copy(s).start()
        return carry

    def wait(s, carry):
        copy(s).wait()
        return carry

    lax.fori_loop(0, live, start, 0)
    for one in copies[2:]:
        one.wait()
    lax.fori_loop(0, live, wait, 0)


def products(order, col_block, tile_ref, parts):
    sub = parts[0].shape[0]
    row = lax.axis_index("row")
    begin = pl.multiple_of((lax.axis_index("col") ^ col_block) * sub, sub)
    total = None
    for k, part in zip(order, parts):
        across = pl.multiple_of((row ^ k) * sub, sub)
        block = tile_ref[pl.ds(begin, sub), pl.ds(across, sub)]
        term = jnp.dot(block, part[...], preferred_element_type=F32)
        total = term if total is None else total + term
    return total


def aggregate_ready(order, n_col, tile_ref, *refs):
    for k in range(n_col):
        refs[-1][k] = products(order, k, tile_ref, refs[:-1])


def aggregate(order, n_col, tile_ref, before_ref, *refs):
    parts = refs[: len(order)]
    keep_ref, *send_refs = refs[len(order) :]
    for k in range(n_col):
        part = before_ref[k] + products(order, k, tile_ref, parts)
        if k < 2:
            keep_ref[k] = part
        else:
            send_refs[k // 2 - 1][k % 2] = part.astype(BF16)


def own_half(rows):
    bits = (lax.axis_index("row"), lax.axis_index("col"))
    parity = 0
    for index, axis in zip(bits, ("row", "col")):
        for b in range(lax.axis_size(axis).bit_length() - 1):
            parity = parity ^ ((index >> b) & 1)
    mine = pl.multiple_of(parity * rows, rows)
    return pl.ds(mine, rows), pl.ds(pl.multiple_of(rows - mine, rows), rows)


def weight_term(n_col, scale, *refs):
    parts = refs[2 : 2 + n_col // 2]
    mine_ref, other_ref, whole = refs[2 + n_col // 2 :]
    total = jnp.zeros(whole.shape, F32)
    for z, part in enumerate(parts):
        for side in range(2):
            term = part[side].astype(BF16)
            total += jnp.dot(refs[side][z].T, term, preferred_element_type=F32)
    whole[...] = total.T * scale
    mine, other = own_half(mine_ref.shape[0])
    mine_ref[...] = whole[mine, :]
    other_ref[...] = whole[other, :]


def finish_weight(mine_ref, other_ref, after_ref, out_ref):
    mine, other = own_half(mine_ref.shape[0])
    out_ref[mine, :] = mine_ref[...]
    out_ref[other, :] = other_ref[...]


def feature_terms(side, cot_ref, tile_ref, weight_ref, *refs):
    total_ref, before_ref = refs[-1], refs[0] if side else None
    deep, sub = cot_ref.shape[:2]
    col = lax.axis_index("col")
    weight = weight_ref[...]
    for z in range(deep):
        begin = pl.multiple_of((col ^ (2 * z + side)) * sub, sub)
        grad = jnp.dot(weight, cot_ref[z].T, preferred_element_type=F32).astype(BF16)
        term = jnp.dot(grad, tile_ref[pl.ds(begin, sub), :], preferred_element_type=F32)
        if z > 0:
            total_ref[...] += term
        elif before_ref is not None:
            total_ref[...] = before_ref[...] + term
        else:
            total_ref[...] = term


def cut(n_row, total_ref, token_ref, after_ref, q_keep, q_send):
    sub = q_keep.shape[2]
    row = lax.axis_index("row")
    for k in range(n_row):
        begin = pl.multiple_of((row ^ k) * sub, sub)
        piece = total_ref[:, pl.ds(begin, sub)]
        if (k + (k > 1)) % 2:
            q_send[k // 2] = piece
        else:
            q_keep[k // 2] = piece


def add_deep(keep_ref, *refs):
    own, other = keep_ref[0], keep_ref[1]
    for ref in refs[:-2]:
        own += ref[0].astype(F32)
        other += ref[1].astype(F32)
    refs[-2][...] = own
    refs[-1][...] = other.astype(BF16)


def add_pairs(keep_ref, got_ref, own_ref, *send_refs):
    own_ref[...] = keep_ref[0] + got_ref[0].astype(F32)
    for k, ref in enumerate(send_refs):
        ref[...] = (keep_ref[k + 1] + got_ref[k + 1].astype(F32)).astype(BF16)


def add_tree(count, *refs):
    half = count // 2
    places = [0, *range(count - half + 1, count), *range(1, count - half + 1)]
    terms = [refs[k][...] for k in places]
    while len(terms) > 1:
        half = len(terms) // 2
        terms = [terms[k] + terms[half + k] for k in range(half)]
    refs[-1][...] = terms[0]


def add_last(count, *refs):
    add_tree(count, *refs[:count], refs[-2])
    refs[-1][...] = (refs[count][...] + refs[count + 1][...].astype(F32)).astype(BF16)


def finish(total_ref, weight_ref, own_ref, *refs):
    out_ref, grad_ref = refs[-2:]
    out_ref[0] = jnp.dot(total_ref[...], weight_ref[...], preferred_element_type=F32).astype(BF16)
    total = own_ref[...]
    for ref in refs[:-2]:
        total += ref[...].astype(F32)
    grad_ref[0] = total.T.astype(BF16)


def local(features, block_values, block_row, block_col, block_occupancy, weight, cotangent):
    n_row, n_col = lax.axis_size("row"), lax.axis_size("col")
    sub, width = features.shape[1:]
    slots, block = block_values.shape[2:4]
    rows, cols = n_col * sub, n_row * sub
    x_own, c_own = features[0], cotangent[0]

    def move(x, axis, k):
        n = lax.axis_size(axis)
        return lax.ppermute(x, axis, [(i, i ^ k) for i in range(n)])

    def far(x):
        return pltpu.with_memory_space_constraint(x, pltpu.HBM)

    deep = n_col // 2
    c_deep = [move(c_own, "col", 2 * k) for k in range(deep - 1, 0, -1)]
    x_far = [move(x_own, "row", k) for k in range(3, n_row, 2)]
    tile, c_near, w_near, x_near = call(
        densify,
        [
            sds((rows, cols), BF16),
            sds((sub, width), BF16),
            sds((width, width), BF16),
            sds((sub, width), BF16),
        ],
        [SMEM] + [HBM] * 6,
        [block_occupancy, *map(far, (block_row, block_col, block_values, c_own, weight, x_own))],
        [
            pltpu.SMEM(block_row.shape, jnp.int32),
            pltpu.SMEM(block_row.shape, jnp.int32),
            pltpu.SemaphoreType.DMA((slots,)),
            pltpu.SemaphoreType.DMA((5,)),
        ],
        name="densify",
    )
    moved = {("c", k): x for k, x in enumerate([c_near, *c_deep[::-1]])}
    moved |= {("x", k): x for k, x in enumerate(x_far)}
    half = deep // 2
    order = [("c", k) for k in [0, *range(half, deep), *range(1, half)]] + list(moved)[deep:]
    c_deep, *x_far = call(
        functools.partial(join, order),
        [sds((deep, sub, width), BF16)] + [sds((sub, width), BF16)] * len(x_far),
        [VMEM] * len(order),
        [moved[key] for key in order],
        name="join",
    )
    c_side = move(c_deep, "col", 1)
    x_parts = [x_near, move(x_own, "row", 1)]
    for x in x_far:
        x_parts += [move(x, "row", 1), x]
    ready = [0, *range(3, n_row, 2)]
    waited = [1, *range(2, n_row, 2)]
    (p_ready,) = call(
        functools.partial(aggregate_ready, ready, n_col),
        [sds((n_col, sub, width), F32)],
        [VMEM] * (1 + len(ready)),
        [tile, *(x_parts[k] for k in ready)],
        flops=rows * cols * width,
        name="aggregate_ready",
    )
    keep, *send = call(
        functools.partial(aggregate, waited, n_col),
        [sds((2, sub, width), F32)] + [sds((2, sub, width), BF16)] * (deep - 1),
        [VMEM] * (2 + len(waited)),
        [tile, p_ready, *(x_parts[k] for k in waited)],
        flops=rows * cols * width,
        name="aggregate",
    )
    got = [move(send[k], "col", 2 * k + 2) for k in range(deep - 2, -1, -1)]
    w_part, w_other = call(
        functools.partial(weight_term, n_col, 1.0 / math.sqrt(n_row * rows)),
        [sds((width // 2, width), F32)] * 2,
        [VMEM] * (2 + deep),
        [c_deep, c_side, keep, *send],
        [pltpu.VMEM((width, width), F32)],
        flops=2 * rows * width * width,
        name="weight_term",
    )
    w_got = move(w_other, "row", 1)
    (w_total,) = call(
        functools.partial(add_tree, 2),
        [sds(w_part.shape, F32)],
        [VMEM] * 2,
        [w_part, w_got],
        name="add_w",
    )
    (q_near,) = call(
        functools.partial(feature_terms, 0),
        [sds((width, cols), F32)],
        [VMEM] * 4,
        [c_deep, tile, w_near, w_total],
        flops=rows * cols * width,
        name="feature_near",
    )
    (q_total,) = call(
        functools.partial(feature_terms, 1),
        [sds((width, cols), F32)],
        [VMEM] * 5,
        [c_side, tile, w_near, q_near, w_total],
        flops=rows * cols * width,
        name="feature_side",
    )
    p_own, p_send = call(
        add_deep,
        [sds((sub, width), F32), sds((sub, width), BF16)],
        [VMEM] * deep,
        [keep, *got],
        name="add_deep",
    )
    p_got = [move(p_send, "col", 1)]
    def turn(x, mask):
        mask ^= n_col * (mask.bit_count() % 2)
        return lax.ppermute(x, ("row", "col"), [(j, j ^ mask) for j in range(n_row * n_col)])

    def add_w(mine, *got, after=()):
        (total,) = call(
            functools.partial(add_tree, 1 + len(got)),
            [sds(mine.shape, F32)],
            [VMEM] * (1 + len(got) + len(after)),
            [mine, *got, *after],
            name="add_w",
        )
        return total

    for i in range(1, n_row.bit_length() - 1):
        w_total = add_w(w_total, turn(w_total, n_col * 2**i), after=[q_total])
    w_total = add_w(w_total, turn(w_total, 1))
    q_keep, q_send = call(
        functools.partial(cut, n_row),
        [sds((n_row // 2, width, sub), F32)] * 2,
        [VMEM] * 3,
        [q_total, w_total, p_own],
        name="cut",
    )
    q_got = move(q_send, "row", 1)
    w_got = [turn(w_total, 2 * k) for k in [*range(half, deep), *range(1, half)]]
    q_own, *q_out = call(
        add_pairs,
        [sds((width, sub), F32)] + [sds((width, sub), BF16)] * len(x_far),
        [VMEM] * 2,
        [q_keep, q_got],
        name="add_core",
    )
    q_in = [move(x, "row", 2 * k + 3) for k, x in enumerate(q_out)]
    w_total, p_total = call(
        functools.partial(add_last, deep),
        [sds(w_total.shape, F32), sds((sub, width), BF16)],
        [VMEM] * (deep + 2),
        [w_total, *w_got, p_own, *p_got],
        name="add_last",
    )

    w_mate = move(w_total, "row", 1)
    out_rows, feature_grad = call(
        finish,
        [sds((1, sub, width), BF16)] * 2,
        [VMEM] * (3 + len(q_in)),
        [p_total, w_near, q_own, *q_in],
        name="finish",
    )
    (weight_grad,) = call(
        finish_weight,
        [sds((width, width), F32)],
        [VMEM] * 2 + [HBM],
        [w_total, w_mate, far(out_rows)],
        name="finish_weight",
    )
    return out_rows, weight_grad, feature_grad


def solution(mesh):
    in_specs = (
        P("col", "row", None),
        P("row", "col", None, None, None),
        P("row", "col", None),
        P("row", "col", None),
        P("row", "col"),
        P(),
        P("row", "col", None),
    )
    out_specs = (P("row", "col", None), P(), P("col", "row", None))
    return jax.shard_map(local, mesh=mesh, in_specs=in_specs, out_specs=out_specs, check_vma=False)
```
